32 devices in a mesh: groups: 2 (over x), gx: 4 (over y, core), gy: 4 (over z).
Axes of the slice: x: 2, y: 2, z: 4, core: 2. Of those that a mesh axis runs over, the one named last changes fastest.
Arguments:
- cell_start: float32 [2, 8, 64, 1024], P(None, None, ('groups', 'gx'), 'gy'), parts along dimension 2, may hold values from -6 to 6
- diffusivity: float32 [2, 8, 64, 1024], P(None, None, ('groups', 'gx'), 'gy'), parts along dimension 2, may hold values from 0.01 to 0.07
- host_cell: int32 [262144], P(('groups', 'gx', 'gy')), parts along dimension 0, may hold values from 0 to 16383
- disp_start: float32 [6, 262144], P(None, ('groups', 'gx', 'gy')), parts along dimension 1, may hold values from -3 to 3
- vel_start: float32 [6, 262144], P(None, ('groups', 'gx', 'gy')), parts along dimension 1, may hold values from -3 to 3
- inertia: float32 [2, 262144], P(None, ('groups', 'gx', 'gy')), parts along dimension 1, may hold values from 1 to 4
- facet_own: int32 [524288], P(('groups', 'gx', 'gy')), parts along dimension 0, may hold values from 0 to 8191
- facet_other: int32 [524288], P(('groups', 'gx', 'gy')), parts along dimension 0, may hold values from 0 to 24575
- facet_arms: float32 [6, 524288], P(None, ('groups', 'gx', 'gy')), parts along dimension 1, may hold values from -3 to 3
- facet_frame: float32 [9, 524288], P(None, ('groups', 'gx', 'gy')), parts along dimension 1, may hold values from -3 to 3
- facet_stiffness: float32 [2, 524288], P(None, ('groups', 'gx', 'gy')), parts along dimension 1, may hold values from 0.2 to 1
- facet_eigen: float32 [2, 524288], P(None, ('groups', 'gx', 'gy')), parts along dimension 1, may hold values from 0.2 to 1
- live_blocks: int32 [32], P(('groups', 'gx', 'gy')), parts along dimension 0, may hold values from 1 to 128, as said below
Outputs:
- cell_state: float32 [2, 8, 64, 1024], P(None, None, ('groups', 'gx'), 'gy'), parts along dimension 2
- particle_disp: float32 [6, 262144], P(None, ('groups', 'gx', 'gy')), parts along dimension 1
- particle_vel: float32 [6, 262144], P(None, ('groups', 'gx', 'gy')), parts along dimension 1
The draws below stay inside these ranges and needn't reach their ends.
There are 2 independent parts, one for each index of `groups`. The reference program is written for one: setup_inputs(seed, part) draws one part's arguments, and reference() takes and returns one part's arrays. A program takes and returns all parts, laid end to end along the dimension named above; each array names one. Nothing has to cross between parts.
Inputs may be any that keep to these rules, and one draw needn't show every extreme that they name: `live_blocks`: partitions with thickness index 0 have all 128 blocks live; others at least a quarter of them.
All inputs are finite; a program needn't handle non-finite values.
Results may differ from the reference program's by a relative error of at most 0.0001.
Values sent between devices are 32-bit elements; how exact they have to be, the bound alone decides.
A program may use at most 128 MiB of HBM per device.

```python
import math
import jax
import jax.numpy as jnp
from jax import lax

CX = 8
LAYERS = 8
P_DEV = 8192
NX = 32
NY = 1024
SLAB = 2
DEVS = 16
NPART = 131072
F_DEV = 16384
NFACET = 262144
FBLOCKS = 128
N_GX = 4
N_GY = 4


def draw_live_blocks(key, part):
    key = jax.random.fold_in(key, 7)
    counts = jax.random.randint(key, (DEVS,), max(1, FBLOCKS // 4), FBLOCKS + 1)
    index_all = jnp.arange(DEVS, dtype=jnp.int32)
    return jnp.where(index_all % N_GY == 0, FBLOCKS, counts).astype(jnp.int32)


def set_ends(result, stream_key, least, top_value):
    dims = result.shape
    spot = [jax.random.randint(jax.random.fold_in(stream_key, axis), (), 0, dims[axis]) for axis in range(len(dims))]
    result = result.at[tuple(spot)].set(least)
    longest = dims.index(max(dims))
    spot[longest] = (spot[longest] + 1) % dims[longest]
    return result.at[tuple(spot)].set(top_value)


def block_scale(key, dims, pieces, low, high):
    factor_of = 1.0
    for position, parts in pieces:
        heights = jax.random.uniform(jax.random.fold_in(jax.random.fold_in(key, 6), position), (parts,), jnp.float32, low / len(pieces), high / len(pieces))
        factor_of = factor_of * jnp.repeat(jnp.exp(heights), dims[position] // parts).reshape((-1,) + (1,) * (len(dims) - 1 - position))
    return factor_of


def noise(rng, dims, deviation, limit, split=(), kind=jnp.bfloat16):
    loudness = block_scale(rng, dims, split, -0.22, 0.18) if split else 1.0
    entries = jax.random.normal(rng, dims, jnp.float32) * deviation * loudness
    return jnp.minimum(jnp.maximum(entries, -limit), limit).astype(kind)


def setup_inputs(seed: int = 0, part: int = 0) -> dict:
    key_of = jax.random.split(jax.random.key(seed), 14)
    own_keys = jax.random.split(jax.random.fold_in(key_of[13], part), 14)
    cell_start = noise(own_keys[0], (2, LAYERS, NX, NY), 1.0, 6.0, ((2, 4), (3, 4)), jnp.float32)
    diffusivity = jnp.clip(jnp.exp(math.log(0.07) - 1.9459102 * jax.random.uniform(own_keys[1], (2, LAYERS, NX, NY), jnp.float32) ** block_scale(own_keys[1], (2, LAYERS, NX, NY), ((2, 4), (3, 4)), -0.2, 0.2)), 0.01, 0.07)
    host_cell = set_ends(jax.random.randint(own_keys[2], (NPART,), 0, SLAB * CX * NY), jax.random.fold_in(own_keys[2], 1), 0, (SLAB * CX * NY) - 1).astype(jnp.int32)
    disp_start = noise(own_keys[3], (6, NPART), 0.5, 3.0, ((1, 16),), jnp.float32)
    vel_start = noise(own_keys[4], (6, NPART), 0.5, 3.0, ((1, 16),), jnp.float32)
    inertia = jnp.clip(jnp.exp(math.log(4.0) - 1.3862944 * jax.random.uniform(own_keys[5], (2, NPART), jnp.float32) ** block_scale(own_keys[5], (2, NPART), ((1, 16),), -0.2, 0.2)), 1.0, 4.0)
    facet_own = set_ends(jax.random.randint(own_keys[6], (NFACET,), 0, P_DEV), jax.random.fold_in(own_keys[6], 1), 0, P_DEV - 1).astype(jnp.int32)
    facet_other = set_ends(jax.random.randint(own_keys[7], (NFACET,), 0, 3 * P_DEV), jax.random.fold_in(own_keys[7], 1), 0, (3 * P_DEV) - 1).astype(jnp.int32)
    facet_arms = noise(own_keys[8], (6, NFACET), 0.5, 3.0, ((1, 16),), jnp.float32)
    facet_frame = noise(own_keys[9], (9, NFACET), 0.6, 3.0, ((1, 16),), jnp.float32)
    facet_stiffness = jnp.clip(jnp.exp(math.log(1.0) - 1.609438 * jax.random.uniform(own_keys[10], (2, NFACET), jnp.float32) ** block_scale(own_keys[10], (2, NFACET), ((1, 16),), -0.2, 0.2)), 0.2, 1.0)
    facet_eigen = jnp.clip(0.2 + 0.8 * jax.random.uniform(own_keys[11], (2, NFACET), jnp.float32) ** block_scale(own_keys[11], (2, NFACET), ((1, 16),), -0.2, 0.2), 0.2, 1.0)
    live_blocks = draw_live_blocks(jax.random.fold_in(jax.random.fold_in(key_of[13], part), 71), part)
    return {"cell_start": cell_start, "diffusivity": diffusivity, "host_cell": host_cell, "disp_start": disp_start, "vel_start": vel_start, "inertia": inertia, "facet_own": facet_own, "facet_other": facet_other, "facet_arms": facet_arms, "facet_frame": facet_frame, "facet_stiffness": facet_stiffness, "facet_eigen": facet_eigen, "live_blocks": live_blocks}


couple_rate = 0.1
time_step = 0.2


def advance(state, rates):
    padded = jnp.pad(state, ((0, 0), (1, 1), (1, 1), (1, 1)))
    center = padded[:, 1:-1, 1:-1, 1:-1]
    laplace = padded[:, 2:, 1:-1, 1:-1] + padded[:, :-2, 1:-1, 1:-1]
    laplace = laplace + padded[:, 1:-1, 2:, 1:-1] + padded[:, 1:-1, :-2, 1:-1]
    laplace = laplace + padded[:, 1:-1, 1:-1, 2:] + padded[:, 1:-1, 1:-1, :-2] - 6.0 * center
    return center + rates * laplace + couple_rate * (center[::-1] - center)


def cross_rows(left, right):
    return jnp.stack([left[1] * right[2] - left[2] * right[1],
                      left[2] * right[0] - left[0] * right[2],
                      left[0] * right[1] - left[1] * right[0]])


def facet_load(own_rows, window, own_idx, other_idx, arms, frame, stiff, eigen, weight_mask):
    side_a = own_rows[:, own_idx]
    side_b = window[:, other_idx]
    arm_a = arms[0:3]
    arm_b = arms[3:6]
    relative = side_b[0:3] + cross_rows(side_b[3:6], arm_b) - side_a[0:3] - cross_rows(side_a[3:6], arm_a)
    strain = [frame[3 * k] * relative[0] + frame[3 * k + 1] * relative[1] + frame[3 * k + 2] * relative[2] for k in range(3)]
    eigen_strain = 0.5 * (eigen[0] * (side_a[7] + side_b[7]) + eigen[1] * (side_a[6] + side_b[6]))
    stress = [stiff[0] * (strain[0] - eigen_strain), stiff[1] * strain[1], stiff[1] * strain[2]]
    force = jnp.stack([stress[0] * frame[m] + stress[1] * frame[3 + m] + stress[2] * frame[6 + m] for m in range(3)])
    moment = cross_rows(arm_a, force)
    terms = jnp.concatenate([force, moment], axis=0) * weight_mask
    segments = own_rows.shape[1]
    return jax.vmap(lambda row: jax.ops.segment_sum(row, own_idx, num_segments=segments))(terms)


def reference(cell_start, diffusivity, host_cell, disp_start, vel_start, inertia, facet_own, facet_other, facet_arms, facet_frame, facet_stiffness, facet_eigen, live_blocks):
    state = cell_start
    for substep in range(3):
        state = advance(state, diffusivity)
    slabs = state.reshape(2, N_GY, SLAB, N_GX, CX, NY)
    slabs = jnp.transpose(slabs, (3, 1, 0, 2, 4, 5)).reshape(DEVS, 2, SLAB * CX * NY)
    hosts = host_cell.reshape(DEVS, P_DEV)
    fields = jax.vmap(lambda slab, host: slab[:, host])(slabs, hosts)
    fields = jnp.transpose(fields, (1, 0, 2)).reshape(2, NPART)
    masses = jnp.repeat(inertia, 3, axis=0)
    blocks = (jnp.arange(F_DEV, dtype=jnp.int32) // 128)[None, :]
    masks = (blocks < live_blocks[:, None]).astype(jnp.float32)
    own_all = facet_own.reshape(DEVS, F_DEV)
    other_all = facet_other.reshape(DEVS, F_DEV)
    arms_all = jnp.transpose(facet_arms.reshape(6, DEVS, F_DEV), (1, 0, 2))
    frame_all = jnp.transpose(facet_frame.reshape(9, DEVS, F_DEV), (1, 0, 2))
    stiff_all = jnp.transpose(facet_stiffness.reshape(2, DEVS, F_DEV), (1, 0, 2))
    eigen_all = jnp.transpose(facet_eigen.reshape(2, DEVS, F_DEV), (1, 0, 2))
    disp = disp_start
    vel = vel_start
    for substep in range(2):
        stacked = jnp.concatenate([disp, fields], axis=0).reshape(8, N_GX, N_GY, P_DEV)
        padded = jnp.pad(stacked, ((0, 0), (1, 1), (0, 0), (0, 0)))
        windows = jnp.concatenate([padded[:, :-2], padded[:, 1:-1], padded[:, 2:]], axis=-1)
        windows = jnp.transpose(windows.reshape(8, DEVS, 3 * P_DEV), (1, 0, 2))
        owners = jnp.transpose(stacked.reshape(8, DEVS, P_DEV), (1, 0, 2))

        def per_device(items):
            return facet_load(*items)

        loads = lax.map(per_device, (owners, windows, own_all, other_all, arms_all, frame_all, stiff_all, eigen_all, masks[:, None, :]))
        loads = jnp.transpose(loads, (1, 0, 2)).reshape(6, NPART)
        vel = vel + time_step * loads / masses
        disp = disp + time_step * vel
    return state, disp, vel
```

```python
import functools
import jax
import jax.numpy as jnp
from jax import lax
from jax.sharding import PartitionSpec as P
from jax.experimental import pallas as pl
from jax.experimental.pallas import tpu as pltpu

couple_rate = 0.1
time_step = 0.2
LANES = 128
GROUP = 4
VMEM_LIMIT = 48 * 1024 * 1024


def padded_2(block, sides, width):
    for axis, dim in sides:
        count = lax.axis_size(axis)
        forward = [(i, i + 1) for i in range(count - 1)]
        backward = [(target, source) for source, target in forward]
        low = lax.ppermute(
            lax.slice_in_dim(block, block.shape[dim] - width, None, axis=dim), axis, forward
        )
        high = lax.ppermute(lax.slice_in_dim(block, 0, width, axis=dim), axis, backward)
        block = jnp.concatenate([low, block, high], axis=dim)
    return block


def neighbours(block, axis):
    count = lax.axis_size(axis)
    forward = [(i, i + 1) for i in range(count - 1)]
    backward = [(target, source) for source, target in forward]
    return lax.ppermute(block, axis, forward), lax.ppermute(block, axis, backward)


def advance_plan(extended, rates):
    padded = jnp.pad(extended, ((0, 0), (1, 1), (0, 0), (0, 0)))
    center = padded[:, 1:-1, 1:-1, 1:-1]
    laplace = padded[:, 2:, 1:-1, 1:-1] + padded[:, :-2, 1:-1, 1:-1]
    laplace = laplace + padded[:, 1:-1, 2:, 1:-1] + padded[:, 1:-1, :-2, 1:-1]
    laplace = laplace + padded[:, 1:-1, 1:-1, 2:] + padded[:, 1:-1, 1:-1, :-2] - 6.0 * center
    return center + rates * laplace + couple_rate * (center[::-1] - center)


def pick(row, lanes):
    return jnp.take_along_axis(row, lanes, axis=1, mode="promise_in_bounds")


def lookup(tables, rows, index_vecs):
    lows = [jnp.bitwise_and(ix, LANES - 1) for ix in index_vecs]
    highs = [lax.shift_right_logical(ix, 7) for ix in index_vecs]
    width = len(index_vecs)
    acc = tuple(jnp.zeros((8, LANES), jnp.float32) for _ in range(rows * width))
    base = 0
    for count, load in tables:
        def step(h, acc, load=load, base=base):
            masks = [hi == h + base for hi in highs]
            out = []
            for r in range(rows):
                row = jnp.broadcast_to(load(r, h), (8, LANES))
                for v in range(width):
                    out.append(jnp.where(masks[v], pick(row, lows[v]), acc[r * width + v]))
            return tuple(out)

        acc = lax.fori_loop(0, count, step, acc, unroll=4)
        base += count
    return [[acc[r * width + v] for v in range(width)] for r in range(rows)]


def flat_table(ref):
    def load(r, h):
        return ref[pl.ds(r, 1), pl.ds(pl.multiple_of(h * LANES, LANES), LANES)]

    return ref.shape[1] // LANES, load


def packed_table(ref):
    def load(r, h):
        return ref[r, pl.ds(h, 1), :]

    return ref.shape[1], load


def cross(left, right):
    return [
        left[1] * right[2] - left[2] * right[1],
        left[2] * right[0] - left[0] * right[2],
        left[0] * right[1] - left[1] * right[0],
    ]


def call(kernel, outs, scratch=(), smem=0, count=0, cost=None):
    specs = [pl.BlockSpec(memory_space=pltpu.SMEM)] * smem
    specs += [pl.BlockSpec(memory_space=pltpu.VMEM)] * (count - smem)
    return pl.pallas_call(
        kernel,
        out_shape=outs,
        in_specs=specs,
        out_specs=jax.tree.map(lambda _: pl.BlockSpec(memory_space=pltpu.VMEM), outs),
        scratch_shapes=list(scratch),
        compiler_params=pltpu.CompilerParams(vmem_limit_bytes=VMEM_LIMIT),
        cost_estimate=cost,
    )


def host_kernel(slab_ref, host_ref, out_ref):
    for g in range(host_ref.shape[0] // (8 * GROUP)):
        index = [host_ref[(g * GROUP + v) * 8:(g * GROUP + v + 1) * 8, :] for v in range(GROUP)]
        found = lookup([packed_table(slab_ref)], 2, index)
        for r in range(2):
            for v in range(GROUP):
                out_ref[r, (g * GROUP + v) * 8:(g * GROUP + v + 1) * 8, :] = found[r][v]


def unpack(src, k0, rows, stage):
    for k in range(8 * GROUP):
        at = pl.multiple_of((k0 + k) * LANES, LANES)
        stage[k * rows:(k + 1) * rows, :] = src[:, pl.ds(at, LANES)]
    return [stage[pl.ds(m, 8 * GROUP, stride=rows), :] for m in range(rows)]


def eigen_kernel(own_f, prev_f, next_f, own_ref, other_ref, eigen_ref, out_ref, stage):
    def chunk(g, carry):
        at = pl.multiple_of(g * 8 * GROUP, 8 * GROUP)
        own_ix = [own_ref[pl.ds(at + 8 * v, 8), :] for v in range(GROUP)]
        oth_ix = [other_ref[pl.ds(at + 8 * v, 8), :] for v in range(GROUP)]
        a = lookup([packed_table(own_f)], 2, own_ix)
        b = lookup([packed_table(prev_f), packed_table(own_f), packed_table(next_f)], 2, oth_ix)
        eig = unpack(eigen_ref, at, 2, stage)
        heat = jnp.concatenate([a[1][v] + b[1][v] for v in range(GROUP)], axis=0)
        pore = jnp.concatenate([a[0][v] + b[0][v] for v in range(GROUP)], axis=0)
        out_ref[pl.ds(at, 8 * GROUP), :] = 0.5 * (eig[0] * heat + eig[1] * pore)
        return carry

    lax.fori_loop(0, own_ref.shape[0] // (8 * GROUP), chunk, 0)


def delta_kernel(own_q, prev_q, next_q, own_ref, other_ref, arms_ref, out_ref, stage):
    def chunk(g, carry):
        at = pl.multiple_of(g * 8 * GROUP, 8 * GROUP)
        own_ix = [own_ref[pl.ds(at + 8 * v, 8), :] for v in range(GROUP)]
        oth_ix = [other_ref[pl.ds(at + 8 * v, 8), :] for v in range(GROUP)]
        join = lambda parts: [jnp.concatenate(row, axis=0) for row in parts]
        a = join(lookup([flat_table(own_q)], 6, own_ix))
        b = join(lookup([flat_table(prev_q), flat_table(own_q), flat_table(next_q)], 6, oth_ix))
        arms = unpack(arms_ref, at, 6, stage)
        turn_a = cross(a[3:6], arms[0:3])
        turn_b = cross(b[3:6], arms[3:6])
        for m in range(3):
            out_ref[m, pl.ds(at, 8 * GROUP), :] = (b[m] + turn_b[m]) - (a[m] + turn_a[m])
        return carry

    lax.fori_loop(0, own_ref.shape[0] // (8 * GROUP), chunk, 0)


def update_kernel(live_ref, delta_ref, eig_ref, own_ref, arms_ref, frame_ref, stiff_ref,
                  inertia_ref, disp_ref, vel_ref, disp_out, vel_out,
                  stage, terms, amat, bmat, total):
    blocks = own_ref.shape[0]
    parts = disp_ref.shape[1]
    low_count = 2 * LANES
    high_count = parts // low_count
    per = 8 * GROUP
    live = live_ref[0]
    total[...] = jnp.zeros_like(total)

    def chunk(g, carry):
        at = pl.multiple_of(g * per, per)
        rows = pl.ds(at, per)
        frame = unpack(frame_ref, at, 9, stage)
        delta = [delta_ref[m, rows, :] for m in range(3)]
        e = [frame[3 * k] * delta[0] + frame[3 * k + 1] * delta[1] + frame[3 * k + 2] * delta[2]
             for k in range(3)]
        stiff = unpack(stiff_ref, at, 2, stage)
        block = at + lax.broadcasted_iota(jnp.int32, (per, LANES), 0)
        weight = jnp.where(block < live, 1.0, 0.0).astype(jnp.float32)
        s = [stiff[0] * (e[0] - eig_ref[rows, :]), stiff[1] * e[1], stiff[1] * e[2]]
        force = [(s[0] * frame[m] + s[1] * frame[3 + m] + s[2] * frame[6 + m]) * weight
                 for m in range(3)]
        arms = unpack(arms_ref, at, 6, stage)
        moment = cross(arms[0:3], force)
        for m in range(3):
            terms[m] = force[m]
            terms[3 + m] = moment[m]

        low_iota = lax.broadcasted_iota(jnp.int32, (low_count, LANES), 0)
        high_iota = lax.broadcasted_iota(jnp.int32, (high_count, LANES), 0)
        for k in range(per):
            lanes = pl.ds(k * LANES, LANES)
            ix = own_ref[pl.ds(at + k, 1), :]
            low = jnp.broadcast_to(jnp.bitwise_and(ix, low_count - 1), (low_count, LANES))
            bmat[:, lanes] = jnp.where(low == low_iota, 1.0, 0.0).astype(jnp.bfloat16)
            here = jnp.broadcast_to(lax.shift_right_logical(ix, 8), (high_count, LANES)) == high_iota
            for m in range(6):
                row = terms[m, k:k + 1, :]
                top = row.astype(jnp.bfloat16).astype(jnp.float32)
                rest = row - top
                at_m = m * high_count
                amat[at_m:at_m + high_count, lanes] = jnp.where(
                    here, jnp.broadcast_to(top, here.shape), 0.0).astype(jnp.bfloat16)
                at_m = (6 + m) * high_count
                amat[at_m:at_m + high_count, lanes] = jnp.where(
                    here, jnp.broadcast_to(rest, here.shape), 0.0).astype(jnp.bfloat16)
        total[...] += lax.dot_general(amat[...], bmat[...], (((1,), (1,)), ((), ())),
                                      preferred_element_type=jnp.float32)
        return carry

    lax.fori_loop(0, blocks // per, chunk, 0)
    half = 6 * high_count
    total[0:half, :] = total[0:half, :] + total[half:2 * half, :]
    for h in range(high_count):
        lanes = pl.ds(h * low_count, low_count)
        load = jnp.concatenate([total[m * high_count + h:m * high_count + h + 1, :] for m in range(6)], axis=0)
        mass = jnp.concatenate([jnp.broadcast_to(inertia_ref[0:1, lanes], (3, low_count)),
                                jnp.broadcast_to(inertia_ref[1:2, lanes], (3, low_count))], axis=0)
        vel = vel_ref[:, lanes] + time_step * load / mass
        vel_out[:, lanes] = vel
        disp_out[:, lanes] = disp_ref[:, lanes] + time_step * vel


def body(
    cell_start,
    diffusivity,
    host_cell,
    disp_start,
    vel_start,
    inertia,
    facet_own,
    facet_other,
    facet_arms,
    facet_frame,
    facet_stiffness,
    facet_eigen,
    live_blocks,
):
    f32 = jnp.float32
    facets = facet_own.shape[0]
    blocks = facets // LANES
    particles = disp_start.shape[1]
    own = facet_own.reshape(blocks, LANES)
    other = facet_other.reshape(blocks, LANES)
    per = 8 * GROUP

    state = cell_start
    for substep in range(3):
        extended = padded_2(state, (("gx", 2), ("gy", 3)), 1)
        state = advance_plan(extended, diffusivity)
    layers = state.shape[1]
    slab_rows = layers // lax.axis_size("gy")
    gathered = lax.all_gather(state, "gy", axis=3, tiled=True)
    slab = lax.dynamic_slice_in_dim(gathered, lax.axis_index("gy") * slab_rows, slab_rows, 1)
    slab = slab.reshape(2, -1, LANES)

    fields = call(host_kernel, jax.ShapeDtypeStruct((2, particles // LANES, LANES), f32), count=2)(
        slab, host_cell.reshape(-1, LANES))
    prev_f, next_f = neighbours(fields, "gx")
    eig = call(eigen_kernel, jax.ShapeDtypeStruct((blocks, LANES), f32), count=6,
               scratch=[pltpu.VMEM((per * 2, LANES), f32)])(
        fields, prev_f, next_f, own, other, facet_eigen)

    disp, vel = disp_start, vel_start
    high_count = particles // (2 * LANES)
    for substep in range(2):
        prev_q, next_q = neighbours(disp, "gx")
        delta = call(delta_kernel, jax.ShapeDtypeStruct((3, blocks, LANES), f32), count=6,
                     scratch=[pltpu.VMEM((per * 6, LANES), f32)])(
            disp, prev_q, next_q, own, other, facet_arms)
        disp, vel = call(
            update_kernel,
            (jax.ShapeDtypeStruct(disp.shape, f32), jax.ShapeDtypeStruct(vel.shape, f32)),
            count=10, smem=1,
            scratch=[
                pltpu.VMEM((per * 9, LANES), f32),
                pltpu.VMEM((6, per, LANES), f32),
                pltpu.VMEM((12 * high_count, per * LANES), jnp.bfloat16),
                pltpu.VMEM((2 * LANES, per * LANES), jnp.bfloat16),
                pltpu.VMEM((12 * high_count, 2 * LANES), f32),
            ])(live_blocks, delta, eig, own, facet_arms, facet_frame, facet_stiffness,
               inertia, disp, vel)
    return (state, disp, vel)


def solution(mesh):
    cells = P(None, None, ("groups", "gx"), "gy")
    vector = P(("groups", "gx", "gy"))
    rows = P(None, ("groups", "gx", "gy"))
    return jax.shard_map(
        body,
        mesh=mesh,
        in_specs=(cells, cells, vector, rows, rows, rows, vector, vector, rows, rows, rows, rows,
                  vector),
        out_specs=(cells, rows, rows),
        check_vma=False,
    )
```

```python
import functools
import jax
import jax.numpy as jnp
from jax import lax
from jax.sharding import PartitionSpec as P
from jax.experimental import pallas as pl
from jax.experimental.pallas import tpu as pltpu

couple_rate = 0.1
time_step = 0.2
LANES = 128
GROUP = 4
VMEM_LIMIT = 48 * 1024 * 1024


def padded_2(block, sides, width):
    for axis, dim in sides:
        count = lax.axis_size(axis)
        forward = [(i, i + 1) for i in range(count - 1)]
        backward = [(target, source) for source, target in forward]
        low = lax.ppermute(
            lax.slice_in_dim(block, block.shape[dim] - width, None, axis=dim), axis, forward
        )
        high = lax.ppermute(lax.slice_in_dim(block, 0, width, axis=dim), axis, backward)
        block = jnp.concatenate([low, block, high], axis=dim)
    return block


def neighbours(block, axis):
    count = lax.axis_size(axis)
    forward = [(i, i + 1) for i in range(count - 1)]
    backward = [(target, source) for source, target in forward]
    return lax.ppermute(block, axis, forward), lax.ppermute(block, axis, backward)


def advance_plan(extended, rates):
    padded = jnp.pad(extended, ((0, 0), (1, 1), (0, 0), (0, 0)))
    center = padded[:, 1:-1, 1:-1, 1:-1]
    laplace = padded[:, 2:, 1:-1, 1:-1] + padded[:, :-2, 1:-1, 1:-1]
    laplace = laplace + padded[:, 1:-1, 2:, 1:-1] + padded[:, 1:-1, :-2, 1:-1]
    laplace = laplace + padded[:, 1:-1, 1:-1, 2:] + padded[:, 1:-1, 1:-1, :-2] - 6.0 * center
    return center + rates * laplace + couple_rate * (center[::-1] - center)


WIDE = 256


def fill_table(table, staged, sources, rows):
    total = staged.shape[0] // rows
    base = 0
    for ref in sources:
        if len(ref.shape) == 3:
            count = ref.shape[1]
            for r in range(rows):
                staged[r * total + base:r * total + base + count, :] = ref[r]
        else:
            count = ref.shape[1] // LANES
            for h in range(count):
                staged[pl.ds(base + h, rows, stride=total), :] = ref[:, h * LANES:(h + 1) * LANES]
        base += count
    value = staged[...]
    top = value.astype(jnp.bfloat16)
    table[:, 0:LANES] = top
    table[:, LANES:2 * LANES] = (value - top.astype(jnp.float32)).astype(jnp.bfloat16)


def look(table, rows, index_row, out, at):
    total = table.shape[0] // rows
    low = jnp.broadcast_to(jnp.bitwise_and(index_row, LANES - 1), (LANES, WIDE))
    hot = jnp.where(low == lax.broadcasted_iota(jnp.int32, (LANES, WIDE), 0), 1.0, 0.0)
    hot = hot.astype(jnp.bfloat16)
    found = jnp.dot(table[...], jnp.concatenate([hot, hot], axis=0), preferred_element_type=jnp.float32)
    high = jnp.broadcast_to(lax.shift_right_logical(index_row, 7), (8, WIDE))
    high = high - lax.broadcasted_iota(jnp.int32, (8, WIDE), 0)
    acc = [jnp.zeros((8, WIDE), jnp.float32) for _ in range(rows)]
    for hb in range(total // 8):
        mask = high == 8 * hb
        for r in range(rows):
            first = r * total + 8 * hb
            acc[r] = jnp.where(mask, found[first:first + 8, :], acc[r])
    for r in range(rows):
        for k in range(WIDE // LANES):
            out[r, pl.ds(at + 8 * k, 8), :] = acc[r][:, k * LANES:(k + 1) * LANES]


def index_of(ref, g):
    per = WIDE // LANES
    return jnp.concatenate([ref[pl.ds(g * per + k, 1), :] for k in range(per)], axis=1)


def gathered_row(out, r, first, count):
    parts = [out[r, pl.ds(first * 8 + s, count, stride=8), :] for s in range(8)]
    while len(parts) > 1:
        parts = [x + y for x, y in zip(parts[::2], parts[1::2])]
    return parts[0]


def cross(left, right):
    return [
        left[1] * right[2] - left[2] * right[1],
        left[2] * right[0] - left[0] * right[2],
        left[0] * right[1] - left[1] * right[0],
    ]


def call(kernel, outs, scratch=(), smem=0, count=0, cost=None):
    specs = [pl.BlockSpec(memory_space=pltpu.SMEM)] * smem
    specs += [pl.BlockSpec(memory_space=pltpu.VMEM)] * (count - smem)
    return pl.pallas_call(
        kernel,
        out_shape=outs,
        in_specs=specs,
        out_specs=jax.tree.map(lambda _: pl.BlockSpec(memory_space=pltpu.VMEM), outs),
        scratch_shapes=list(scratch),
        compiler_params=pltpu.CompilerParams(vmem_limit_bytes=VMEM_LIMIT),
        cost_estimate=cost,
    )


def host_kernel(slab_ref, host_ref, out_ref, staged, table, found):
    fill_table(table, staged, [slab_ref], 2)

    def chunk(g, carry):
        look(table, 2, index_of(host_ref, g), found, pl.multiple_of(g * 8 * (WIDE // LANES), 8))
        return carry

    blocks = host_ref.shape[0]
    lax.fori_loop(0, blocks * LANES // WIDE, chunk, 0)
    for r in range(2):
        out_ref[r] = gathered_row(found, r, 0, blocks)


def unpack(src, k0, rows, stage):
    for k in range(8 * GROUP):
        at = pl.multiple_of((k0 + k) * LANES, LANES)
        stage[k * rows:(k + 1) * rows, :] = src[:, pl.ds(at, LANES)]
    return [stage[pl.ds(m, 8 * GROUP, stride=rows), :] for m in range(rows)]


def find_both(rows, own_ref, other_ref, own_q, prev_q, next_q, scratch):
    staged_a, table_a, found_a, staged_b, table_b, found_b = scratch
    fill_table(table_a, staged_a, [own_q], rows)
    fill_table(table_b, staged_b, [prev_q, own_q, next_q], rows)

    def chunk(g, carry):
        at = pl.multiple_of(g * 8 * (WIDE // LANES), 8)
        look(table_a, rows, index_of(own_ref, g), found_a, at)
        look(table_b, rows, index_of(other_ref, g), found_b, at)
        return carry

    lax.fori_loop(0, own_ref.shape[0] * LANES // WIDE, chunk, 0)
    return found_a, found_b


def eigen_kernel(own_f, prev_f, next_f, own_ref, other_ref, eigen_ref, out_ref, stage, *scratch):
    found_a, found_b = find_both(2, own_ref, other_ref, own_f, prev_f, next_f, scratch)

    def chunk(g, carry):
        at = pl.multiple_of(g * 8 * GROUP, 8 * GROUP)
        eig = unpack(eigen_ref, at, 2, stage)
        pore, heat = [
            gathered_row(found_a, r, at, 8 * GROUP) + gathered_row(found_b, r, at, 8 * GROUP)
            for r in range(2)]
        out_ref[pl.ds(at, 8 * GROUP), :] = 0.5 * (eig[0] * heat + eig[1] * pore)
        return carry

    lax.fori_loop(0, own_ref.shape[0] // (8 * GROUP), chunk, 0)


def delta_kernel(own_q, prev_q, next_q, own_ref, other_ref, arms_ref, out_ref, stage, *scratch):
    found_a, found_b = find_both(6, own_ref, other_ref, own_q, prev_q, next_q, scratch)

    def chunk(g, carry):
        at = pl.multiple_of(g * 8 * GROUP, 8 * GROUP)
        a = [gathered_row(found_a, r, at, 8 * GROUP) for r in range(6)]
        b = [gathered_row(found_b, r, at, 8 * GROUP) for r in range(6)]
        arms = unpack(arms_ref, at, 6, stage)
        turn_a = cross(a[3:6], arms[0:3])
        turn_b = cross(b[3:6], arms[3:6])
        for m in range(3):
            out_ref[m, pl.ds(at, 8 * GROUP), :] = (b[m] + turn_b[m]) - (a[m] + turn_a[m])
        return carry

    lax.fori_loop(0, own_ref.shape[0] // (8 * GROUP), chunk, 0)


def update_kernel(live_ref, delta_ref, eig_ref, own_ref, arms_ref, frame_ref, stiff_ref,
                  inertia_ref, disp_ref, vel_ref, disp_out, vel_out,
                  stage, terms, amat, bmat, total):
    blocks = own_ref.shape[0]
    parts = disp_ref.shape[1]
    low_count = 2 * LANES
    high_count = parts // low_count
    per = 8 * GROUP
    live = live_ref[0]
    total[...] = jnp.zeros_like(total)

    def chunk(g, carry):
        at = pl.multiple_of(g * per, per)
        rows = pl.ds(at, per)
        frame = unpack(frame_ref, at, 9, stage)
        delta = [delta_ref[m, rows, :] for m in range(3)]
        e = [frame[3 * k] * delta[0] + frame[3 * k + 1] * delta[1] + frame[3 * k + 2] * delta[2]
             for k in range(3)]
        stiff = unpack(stiff_ref, at, 2, stage)
        block = at + lax.broadcasted_iota(jnp.int32, (per, LANES), 0)
        weight = jnp.where(block < live, 1.0, 0.0).astype(jnp.float32)
        s = [stiff[0] * (e[0] - eig_ref[rows, :]), stiff[1] * e[1], stiff[1] * e[2]]
        force = [(s[0] * frame[m] + s[1] * frame[3 + m] + s[2] * frame[6 + m]) * weight
                 for m in range(3)]
        arms = unpack(arms_ref, at, 6, stage)
        moment = cross(arms[0:3], force)
        for m in range(3):
            terms[m] = force[m]
            terms[3 + m] = moment[m]

        low_iota = lax.broadcasted_iota(jnp.int32, (low_count, LANES), 0)
        high_iota = lax.broadcasted_iota(jnp.int32, (high_count, LANES), 0)
        for k in range(per):
            lanes = pl.ds(k * LANES, LANES)
            ix = own_ref[pl.ds(at + k, 1), :]
            low = jnp.broadcast_to(jnp.bitwise_and(ix, low_count - 1), (low_count, LANES))
            bmat[:, lanes] = jnp.where(low == low_iota, 1.0, 0.0).astype(jnp.bfloat16)
            here = jnp.broadcast_to(lax.shift_right_logical(ix, 8), (high_count, LANES)) == high_iota
            for m in range(6):
                row = terms[m, k:k + 1, :]
                top = row.astype(jnp.bfloat16).astype(jnp.float32)
                rest = row - top
                at_m = m * high_count
                amat[at_m:at_m + high_count, lanes] = jnp.where(
                    here, jnp.broadcast_to(top, here.shape), 0.0).astype(jnp.bfloat16)
                at_m = (6 + m) * high_count
                amat[at_m:at_m + high_count, lanes] = jnp.where(
                    here, jnp.broadcast_to(rest, here.shape), 0.0).astype(jnp.bfloat16)
        total[...] += lax.dot_general(amat[...], bmat[...], (((1,), (1,)), ((), ())),
                                      preferred_element_type=jnp.float32)
        return carry

    lax.fori_loop(0, blocks // per, chunk, 0)
    half = 6 * high_count
    total[0:half, :] = total[0:half, :] + total[half:2 * half, :]
    for h in range(high_count):
        lanes = pl.ds(h * low_count, low_count)
        load = jnp.concatenate([total[m * high_count + h:m * high_count + h + 1, :] for m in range(6)], axis=0)
        mass = jnp.concatenate([jnp.broadcast_to(inertia_ref[0:1, lanes], (3, low_count)),
                                jnp.broadcast_to(inertia_ref[1:2, lanes], (3, low_count))], axis=0)
        vel = vel_ref[:, lanes] + time_step * load / mass
        vel_out[:, lanes] = vel
        disp_out[:, lanes] = disp_ref[:, lanes] + time_step * vel


def body(
    cell_start,
    diffusivity,
    host_cell,
    disp_start,
    vel_start,
    inertia,
    facet_own,
    facet_other,
    facet_arms,
    facet_frame,
    facet_stiffness,
    facet_eigen,
    live_blocks,
):
    f32 = jnp.float32
    facets = facet_own.shape[0]
    blocks = facets // LANES
    particles = disp_start.shape[1]
    own = facet_own.reshape(blocks, LANES)
    other = facet_other.reshape(blocks, LANES)
    per = 8 * GROUP

    state = cell_start
    for substep in range(3):
        extended = padded_2(state, (("gx", 2), ("gy", 3)), 1)
        state = advance_plan(extended, diffusivity)
    layers = state.shape[1]
    slab_rows = layers // lax.axis_size("gy")
    gathered = lax.all_gather(state, "gy", axis=3, tiled=True)
    slab = lax.dynamic_slice_in_dim(gathered, lax.axis_index("gy") * slab_rows, slab_rows, 1)
    slab = slab.reshape(2, -1, LANES)

    def tables(rows, high, found):
        return [pltpu.VMEM((rows * high, LANES), f32),
                pltpu.VMEM((rows * high, 2 * LANES), jnp.bfloat16),
                pltpu.VMEM((rows, 8 * found, LANES), f32)]

    high = particles // LANES
    fields = call(host_kernel, jax.ShapeDtypeStruct((2, high, LANES), f32), count=2,
                  scratch=tables(2, slab.shape[1], high))(
        slab, host_cell.reshape(-1, LANES))
    prev_f, next_f = neighbours(fields, "gx")
    eig = call(eigen_kernel, jax.ShapeDtypeStruct((blocks, LANES), f32), count=6,
               scratch=[pltpu.VMEM((per * 2, LANES), f32)] + tables(2, high, blocks)
               + tables(2, 3 * high, blocks))(
        fields, prev_f, next_f, own, other, facet_eigen)

    disp, vel = disp_start, vel_start
    high_count = particles // (2 * LANES)
    for substep in range(2):
        prev_q, next_q = neighbours(disp, "gx")
        delta = call(delta_kernel, jax.ShapeDtypeStruct((3, blocks, LANES), f32), count=6,
                     scratch=[pltpu.VMEM((per * 6, LANES), f32)] + tables(6, high, blocks)
                     + tables(6, 3 * high, blocks))(
            disp, prev_q, next_q, own, other, facet_arms)
        disp, vel = call(
            update_kernel,
            (jax.ShapeDtypeStruct(disp.shape, f32), jax.ShapeDtypeStruct(vel.shape, f32)),
            count=10, smem=1,
            scratch=[
                pltpu.VMEM((per * 9, LANES), f32),
                pltpu.VMEM((6, per, LANES), f32),
                pltpu.VMEM((12 * high_count, per * LANES), jnp.bfloat16),
                pltpu.VMEM((2 * LANES, per * LANES), jnp.bfloat16),
                pltpu.VMEM((12 * high_count, 2 * LANES), f32),
            ])(live_blocks, delta, eig, own, facet_arms, facet_frame, facet_stiffness,
               inertia, disp, vel)
    return (state, disp, vel)


def solution(mesh):
    cells = P(None, None, ("groups", "gx"), "gy")
    vector = P(("groups", "gx", "gy"))
    rows = P(None, ("groups", "gx", "gy"))
    return jax.shard_map(
        body,
        mesh=mesh,
        in_specs=(cells, cells, vector, rows, rows, rows, vector, vector, rows, rows, rows, rows,
                  vector),
        out_specs=(cells, rows, rows),
        check_vma=False,
    )
```

```python
import functools
import jax
import jax.numpy as jnp
from jax import lax
from jax.sharding import PartitionSpec as P
from jax.experimental import pallas as pl
from jax.experimental.pallas import tpu as pltpu

couple_rate = 0.1
time_step = 0.2
LANES = 128
GROUP = 4
VMEM_LIMIT = 48 * 1024 * 1024


def neighbours(block, axis):
    count = lax.axis_size(axis)
    forward = [(i, i + 1) for i in range(count - 1)]
    backward = [(target, source) for source, target in forward]
    return lax.ppermute(block, axis, forward), lax.ppermute(block, axis, backward)


def flow_kernel(cell_ref, rate_ref, disp_ref, state_out, slab_out, prev_out, next_out,
                held, crest_edge, crest_halo, plan_halo,
                crest_send, crest_recv, plan_send, plan_recv, disp_send, disp_recv,
                slab_send, slab_recv):
    x, y = lax.axis_index("gx"), lax.axis_index("gy")
    nx, ny = lax.axis_size("gx"), lax.axis_size("gy")
    rows, layers, crest, thick = cell_ref.shape
    slab = layers // ny
    has_lo, has_hi = (x > 0, y > 0), (x < nx - 1, y < ny - 1)

    barrier = pltpu.get_barrier_semaphore()

    def greet(axis, target):
        pl.semaphore_signal(barrier, inc=1, device_id={axis: target},
                            device_id_type=pl.DeviceIdType.MESH)

    @pl.when(has_lo[0])
    def _():
        greet("gx", x - 1)

    @pl.when(has_hi[0])
    def _():
        greet("gx", x + 1)

    for o in range(1, ny):
        greet("gy", lax.rem(y + o, ny))
    greeted = jnp.where(has_lo[0], 1, 0) + jnp.where(has_hi[0], 1, 0) + (ny - 1)
    pl.semaphore_wait(barrier, greeted)

    def remote(src, dst, send, recv, axis, target):
        return pltpu.make_async_remote_copy(
            src_ref=src, dst_ref=dst, send_sem=send, recv_sem=recv,
            device_id={axis: target}, device_id_type=pl.DeviceIdType.MESH)

    def both_ways(axis, lo_src, hi_src, lo_dst, hi_dst, send, recv):
        at, i = (x, 0) if axis == "gx" else (y, 1)
        down = remote(lo_src, hi_dst, send.at[0], recv.at[0], axis, at - 1)
        up = remote(hi_src, lo_dst, send.at[1], recv.at[1], axis, at + 1)
        return has_lo[i], has_hi[i], down, up, lo_dst, hi_dst

    def start(pair):
        lo, hi, down, up, lo_dst, hi_dst = pair

        @pl.when(lo)
        def _():
            down.start()

        @pl.when(hi)
        def _():
            up.start()

        @pl.when(jnp.logical_not(lo))
        def _():
            lo_dst[...] = jnp.zeros_like(lo_dst)

        @pl.when(jnp.logical_not(hi))
        def _():
            hi_dst[...] = jnp.zeros_like(hi_dst)

    def finish(pair):
        lo, hi, down, up, _, _ = pair

        @pl.when(lo)
        def _():
            down.wait_send()
            up.wait_recv()

        @pl.when(hi)
        def _():
            up.wait_send()
            down.wait_recv()

    states = [cell_ref, held.at[0], held.at[1], state_out]
    lane = lax.broadcasted_iota(jnp.int32, (crest, thick), 1)
    line = lax.broadcasted_iota(jnp.int32, (crest, thick), 0)
    whole = (crest, thick)
    disp_pair = both_ways("gx", disp_ref, disp_ref, prev_out, next_out, disp_send, disp_recv)
    for step in range(3):
        now, later = states[step], states[step + 1]
        for r in range(rows):
            for l in range(layers):
                crest_edge[step, 0, r, l:l + 1, :] = now[r, l, 0:1, :]
                crest_edge[step, 1, r, l:l + 1, :] = now[r, l, crest - 1:crest, :]
        crest_pair = both_ways("gx", crest_edge.at[step, 0], crest_edge.at[step, 1],
                               crest_halo.at[step, 0], crest_halo.at[step, 1],
                               crest_send.at[step], crest_recv.at[step])
        plan_pair = both_ways("gy", now.at[:, :, :, 0:LANES], now.at[:, :, :, thick - LANES:thick],
                              plan_halo.at[step, 0], plan_halo.at[step, 1],
                              plan_send.at[step], plan_recv.at[step])
        start(plan_pair)
        start(crest_pair)
        if step == 0:
            start(disp_pair)
        finish(plan_pair)
        finish(crest_pair)
        for l in range(layers):
            center = [now[r, l] for r in range(rows)]
            for r in range(rows):
                c = center[r]
                none = jnp.zeros_like(c)
                lap = (now[r, l + 1] if l + 1 < layers else none) + (now[r, l - 1] if l > 0 else none)
                lap += jnp.where(line == crest - 1,
                                 jnp.broadcast_to(crest_halo[step, 1, r, l:l + 1, :], whole),
                                 pltpu.roll(c, crest - 1, 0))
                lap += jnp.where(line == 0,
                                 jnp.broadcast_to(crest_halo[step, 0, r, l:l + 1, :], whole),
                                 pltpu.roll(c, 1, 0))
                hi_col = plan_halo[step, 1, r, l][:, 0:1]
                lo_col = plan_halo[step, 0, r, l][:, LANES - 1:LANES]
                lap += jnp.where(lane == thick - 1, jnp.broadcast_to(hi_col, whole),
                                 pltpu.roll(c, thick - 1, 1))
                lap += jnp.where(lane == 0, jnp.broadcast_to(lo_col, whole), pltpu.roll(c, 1, 1))
                lap -= 6.0 * c
                later[r, l] = c + rate_ref[r, l] * lap + couple_rate * (center[1 - r] - c)

    copies = []
    for o in range(1, ny):
        target = lax.rem(y + o, ny)
        copies.append(remote(state_out.at[:, pl.ds(target * slab, slab)], slab_out.at[y],
                             slab_send.at[o - 1], slab_recv.at[o - 1], "gy", target))
    for copy in copies:
        copy.start()
    slab_out[y] = state_out[:, pl.ds(y * slab, slab)]
    for copy in copies:
        copy.wait()
    finish(disp_pair)


WIDE = 256


def stage_rows(staged, sources, first, total):
    base = 0
    for ref in sources:
        rows = ref.shape[0]
        if len(ref.shape) == 3:
            count = ref.shape[1]
            for r in range(rows):
                at = (first + r) * total + base
                staged[at:at + count, :] = ref[r]
        else:
            count = ref.shape[1] // LANES
            for h in range(count):
                staged[pl.ds(first * total + base + h, rows, stride=total), :] = (
                    ref[:, h * LANES:(h + 1) * LANES])
        base += count


def split_table(table, staged):
    value = staged[...]
    top = value.astype(jnp.bfloat16)
    table[:, 0:LANES] = top
    table[:, LANES:2 * LANES] = (value - top.astype(jnp.float32)).astype(jnp.bfloat16)


def look(table, rows, index_row, out, at):
    total = table.shape[0] // rows
    low = jnp.broadcast_to(jnp.bitwise_and(index_row, LANES - 1), (LANES, WIDE))
    hot = jnp.where(low == lax.broadcasted_iota(jnp.int32, (LANES, WIDE), 0), 1.0, 0.0)
    hot = hot.astype(jnp.bfloat16)
    found = jnp.dot(table[...], jnp.concatenate([hot, hot], axis=0), preferred_element_type=jnp.float32)
    high = jnp.broadcast_to(lax.shift_right_logical(index_row, 7), (8, WIDE))
    high = high - lax.broadcasted_iota(jnp.int32, (8, WIDE), 0)
    acc = [jnp.zeros((8, WIDE), jnp.float32) for _ in range(rows)]
    for hb in range(total // 8):
        mask = high == 8 * hb
        for r in range(rows):
            first = r * total + 8 * hb
            acc[r] = jnp.where(mask, found[first:first + 8, :], acc[r])
    for r in range(rows):
        for k in range(WIDE // LANES):
            out[r, pl.ds(at + 8 * k, 8), :] = acc[r][:, k * LANES:(k + 1) * LANES]


def index_of(ref, g):
    per = WIDE // LANES
    return jnp.concatenate([ref[pl.ds(g * per + k, 1), :] for k in range(per)], axis=1)


def gathered_row(out, r, first, count):
    parts = [out[r, pl.ds(first * 8 + s, count, stride=8), :] for s in range(8)]
    while len(parts) > 1:
        parts = [x + y for x, y in zip(parts[::2], parts[1::2])]
    return parts[0]


def cross(left, right):
    return [
        left[1] * right[2] - left[2] * right[1],
        left[2] * right[0] - left[0] * right[2],
        left[0] * right[1] - left[1] * right[0],
    ]


def call(kernel, outs, scratch=(), smem=0, count=0, cost=None):
    specs = [pl.BlockSpec(memory_space=pltpu.SMEM)] * smem
    specs += [pl.BlockSpec(memory_space=pltpu.VMEM)] * (count - smem)
    return pl.pallas_call(
        kernel,
        out_shape=outs,
        in_specs=specs,
        out_specs=jax.tree.map(lambda _: pl.BlockSpec(memory_space=pltpu.VMEM), outs),
        scratch_shapes=list(scratch),
        compiler_params=pltpu.CompilerParams(vmem_limit_bytes=VMEM_LIMIT),
        cost_estimate=cost,
    )


def host_kernel(slab_ref, host_ref, out_ref, staged, table, found):
    sources, _, layers, crest, thick = slab_ref.shape
    pieces = thick // LANES
    line = sources * pieces
    for j in range(sources):
        for r in range(2):
            for l in range(layers):
                for p in range(pieces):
                    at = ((r * layers + l) * crest) * line + j * pieces + p
                    staged[pl.ds(at, crest, stride=line), :] = (
                        slab_ref[j, r, l, :, p * LANES:(p + 1) * LANES])
    split_table(table, staged)

    def chunk(g, carry):
        look(table, 2, index_of(host_ref, g), found, pl.multiple_of(g * 8 * (WIDE // LANES), 8))
        return carry

    blocks = host_ref.shape[0]
    lax.fori_loop(0, blocks * LANES // WIDE, chunk, 0)
    for r in range(2):
        out_ref[r] = gathered_row(found, r, 0, blocks)


def unpack(src, k0, rows, stage):
    for k in range(8 * GROUP):
        at = pl.multiple_of((k0 + k) * LANES, LANES)
        stage[k * rows:(k + 1) * rows, :] = src[:, pl.ds(at, LANES)]
    return [stage[pl.ds(m, 8 * GROUP, stride=rows), :] for m in range(rows)]


def find_both(own_ref, other_ref, owners, windows, scratch):
    staged_a, table_a, found_a, staged_b, table_b, found_b = scratch
    rows = sum(ref.shape[0] for ref in owners)
    first = 0
    for ref, three in zip(owners, windows):
        stage_rows(staged_a, [ref], first, staged_a.shape[0] // rows)
        stage_rows(staged_b, three, first, staged_b.shape[0] // rows)
        first += ref.shape[0]
    split_table(table_a, staged_a)
    split_table(table_b, staged_b)

    def chunk(g, carry):
        at = pl.multiple_of(g * 8 * (WIDE // LANES), 8)
        look(table_a, rows, index_of(own_ref, g), found_a, at)
        look(table_b, rows, index_of(other_ref, g), found_b, at)
        return carry

    lax.fori_loop(0, own_ref.shape[0] * LANES // WIDE, chunk, 0)
    return found_a, found_b


def delta_at(found_a, found_b, arms_ref, out_ref, stage, at):
    a = [gathered_row(found_a, r, at, 8 * GROUP) for r in range(6)]
    b = [gathered_row(found_b, r, at, 8 * GROUP) for r in range(6)]
    arms = unpack(arms_ref, at, 6, stage)
    turn_a = cross(a[3:6], arms[0:3])
    turn_b = cross(b[3:6], arms[3:6])
    for m in range(3):
        out_ref[m, pl.ds(at, 8 * GROUP), :] = (b[m] + turn_b[m]) - (a[m] + turn_a[m])


def first_kernel(own_q, prev_q, next_q, own_f, prev_f, next_f, own_ref, other_ref, arms_ref,
                 eigen_ref, out_ref, eig_ref, stage, *scratch):
    found_a, found_b = find_both(own_ref, other_ref, [own_q, own_f],
                                 [[prev_q, own_q, next_q], [prev_f, own_f, next_f]], scratch)

    def chunk(g, carry):
        at = pl.multiple_of(g * 8 * GROUP, 8 * GROUP)
        delta_at(found_a, found_b, arms_ref, out_ref, stage, at)
        eig = unpack(eigen_ref, at, 2, stage)
        pore, heat = [
            gathered_row(found_a, r, at, 8 * GROUP) + gathered_row(found_b, r, at, 8 * GROUP)
            for r in (6, 7)]
        eig_ref[pl.ds(at, 8 * GROUP), :] = 0.5 * (eig[0] * heat + eig[1] * pore)
        return carry

    lax.fori_loop(0, own_ref.shape[0] // (8 * GROUP), chunk, 0)


def delta_kernel(own_q, prev_q, next_q, own_ref, other_ref, arms_ref, out_ref, stage, *scratch):
    found_a, found_b = find_both(own_ref, other_ref, [own_q], [[prev_q, own_q, next_q]], scratch)

    def chunk(g, carry):
        delta_at(found_a, found_b, arms_ref, out_ref, stage, pl.multiple_of(g * 8 * GROUP, 8 * GROUP))
        return carry

    lax.fori_loop(0, own_ref.shape[0] // (8 * GROUP), chunk, 0)


def update_kernel(live_ref, delta_ref, eig_ref, own_ref, arms_ref, frame_ref, stiff_ref,
                  inertia_ref, disp_ref, vel_ref, disp_out, vel_out,
                  stage, terms, amat, bmat, total):
    blocks = own_ref.shape[0]
    parts = disp_ref.shape[1]
    low_count = 2 * LANES
    high_count = parts // low_count
    per = 8 * GROUP
    live = live_ref[0]
    total[...] = jnp.zeros_like(total)

    def chunk(g, carry):
        at = pl.multiple_of(g * per, per)
        rows = pl.ds(at, per)
        frame = unpack(frame_ref, at, 9, stage)
        delta = [delta_ref[m, rows, :] for m in range(3)]
        e = [frame[3 * k] * delta[0] + frame[3 * k + 1] * delta[1] + frame[3 * k + 2] * delta[2]
             for k in range(3)]
        stiff = unpack(stiff_ref, at, 2, stage)
        block = at + lax.broadcasted_iota(jnp.int32, (per, LANES), 0)
        weight = jnp.where(block < live, 1.0, 0.0).astype(jnp.float32)
        s = [stiff[0] * (e[0] - eig_ref[rows, :]), stiff[1] * e[1], stiff[1] * e[2]]
        force = [(s[0] * frame[m] + s[1] * frame[3 + m] + s[2] * frame[6 + m]) * weight
                 for m in range(3)]
        arms = unpack(arms_ref, at, 6, stage)
        moment = cross(arms[0:3], force)
        for m in range(3):
            terms[m] = force[m]
            terms[3 + m] = moment[m]

        low_iota = lax.broadcasted_iota(jnp.int32, (low_count, LANES), 0)
        high_iota = lax.broadcasted_iota(jnp.int32, (high_count, LANES), 0)
        for k in range(per):
            lanes = pl.ds(k * LANES, LANES)
            ix = own_ref[pl.ds(at + k, 1), :]
            low = jnp.broadcast_to(jnp.bitwise_and(ix, low_count - 1), (low_count, LANES))
            bmat[:, lanes] = jnp.where(low == low_iota, 1.0, 0.0).astype(jnp.bfloat16)
            here = jnp.broadcast_to(lax.shift_right_logical(ix, 8), (high_count, LANES)) == high_iota
            for m in range(6):
                row = terms[m, k:k + 1, :]
                top = row.astype(jnp.bfloat16).astype(jnp.float32)
                rest = row - top
                at_m = m * high_count
                amat[at_m:at_m + high_count, lanes] = jnp.where(
                    here, jnp.broadcast_to(top, here.shape), 0.0).astype(jnp.bfloat16)
                at_m = (6 + m) * high_count
                amat[at_m:at_m + high_count, lanes] = jnp.where(
                    here, jnp.broadcast_to(rest, here.shape), 0.0).astype(jnp.bfloat16)
        total[...] += lax.dot_general(amat[...], bmat[...], (((1,), (1,)), ((), ())),
                                      preferred_element_type=jnp.float32)
        return carry

    lax.fori_loop(0, blocks // per, chunk, 0)
    half = 6 * high_count
    total[0:half, :] = total[0:half, :] + total[half:2 * half, :]
    for h in range(high_count):
        lanes = pl.ds(h * low_count, low_count)
        load = jnp.concatenate([total[m * high_count + h:m * high_count + h + 1, :] for m in range(6)], axis=0)
        mass = jnp.concatenate([jnp.broadcast_to(inertia_ref[0:1, lanes], (3, low_count)),
                                jnp.broadcast_to(inertia_ref[1:2, lanes], (3, low_count))], axis=0)
        vel = vel_ref[:, lanes] + time_step * load / mass
        vel_out[:, lanes] = vel
        disp_out[:, lanes] = disp_ref[:, lanes] + time_step * vel


def body(
    cell_start,
    diffusivity,
    host_cell,
    disp_start,
    vel_start,
    inertia,
    facet_own,
    facet_other,
    facet_arms,
    facet_frame,
    facet_stiffness,
    facet_eigen,
    live_blocks,
):
    f32 = jnp.float32
    facets = facet_own.shape[0]
    blocks = facets // LANES
    particles = disp_start.shape[1]
    own = facet_own.reshape(blocks, LANES)
    other = facet_other.reshape(blocks, LANES)
    per = 8 * GROUP

    ny = lax.axis_size("gy")
    rows, layers, crest, thick = cell_start.shape
    dma = pltpu.SemaphoreType.DMA
    shape = lambda *dims: jax.ShapeDtypeStruct(dims, f32)
    vmem = pl.BlockSpec(memory_space=pltpu.VMEM)
    state, slab, prev_q, next_q = pl.pallas_call(
        flow_kernel,
        out_shape=(shape(*cell_start.shape), shape(ny, rows, layers // ny, crest, thick),
                   shape(*disp_start.shape), shape(*disp_start.shape)),
        in_specs=[vmem] * 3,
        out_specs=(vmem,) * 4,
        scratch_shapes=[
            pltpu.VMEM((2,) + cell_start.shape, f32),
            pltpu.VMEM((3, 2, rows, layers, thick), f32),
            pltpu.VMEM((3, 2, rows, layers, thick), f32),
            pltpu.VMEM((3, 2, rows, layers, crest, LANES), f32),
            dma((3, 2)), dma((3, 2)), dma((3, 2)), dma((3, 2)), dma((2,)), dma((2,)),
            dma((ny - 1,)), dma((ny - 1,)),
        ],
        compiler_params=pltpu.CompilerParams(
            vmem_limit_bytes=VMEM_LIMIT, collective_id=0, has_side_effects=True),
    )(cell_start, diffusivity, disp_start)

    def tables(rows, high, found):
        return [pltpu.VMEM((rows * high, LANES), f32),
                pltpu.VMEM((rows * high, 2 * LANES), jnp.bfloat16),
                pltpu.VMEM((rows, 8 * found, LANES), f32)]

    high = particles // LANES
    fields = call(host_kernel, jax.ShapeDtypeStruct((2, high, LANES), f32), count=2,
                  scratch=tables(2, slab.size // (2 * LANES), high))(
        slab, host_cell.reshape(-1, LANES))
    prev_f, next_f = neighbours(fields, "gx")
    delta, eig = call(first_kernel, (shape(3, blocks, LANES), shape(blocks, LANES)), count=10,
                      scratch=[pltpu.VMEM((per * 6, LANES), f32)] + tables(8, high, blocks)
                      + tables(8, 3 * high, blocks))(
        disp_start, prev_q, next_q, fields, prev_f, next_f, own, other, facet_arms, facet_eigen)

    disp, vel = disp_start, vel_start
    high_count = particles // (2 * LANES)
    for substep in range(2):
        if substep > 0:
            prev_q, next_q = neighbours(disp, "gx")
            delta = call(delta_kernel, jax.ShapeDtypeStruct((3, blocks, LANES), f32), count=6,
                         scratch=[pltpu.VMEM((per * 6, LANES), f32)] + tables(6, high, blocks)
                         + tables(6, 3 * high, blocks))(
                disp, prev_q, next_q, own, other, facet_arms)
        disp, vel = call(
            update_kernel,
            (jax.ShapeDtypeStruct(disp.shape, f32), jax.ShapeDtypeStruct(vel.shape, f32)),
            count=10, smem=1,
            scratch=[
                pltpu.VMEM((per * 9, LANES), f32),
                pltpu.VMEM((6, per, LANES), f32),
                pltpu.VMEM((12 * high_count, per * LANES), jnp.bfloat16),
                pltpu.VMEM((2 * LANES, per * LANES), jnp.bfloat16),
                pltpu.VMEM((12 * high_count, 2 * LANES), f32),
            ])(live_blocks, delta, eig, own, facet_arms, facet_frame, facet_stiffness,
               inertia, disp, vel)
    return (state, disp, vel)


def solution(mesh):
    cells = P(None, None, ("groups", "gx"), "gy")
    vector = P(("groups", "gx", "gy"))
    rows = P(None, ("groups", "gx", "gy"))
    return jax.shard_map(
        body,
        mesh=mesh,
        in_specs=(cells, cells, vector, rows, rows, rows, vector, vector, rows, rows, rows, rows,
                  vector),
        out_specs=(cells, rows, rows),
        check_vma=False,
    )
```

```python
import functools
import jax
import jax.numpy as jnp
from jax import lax
from jax.sharding import PartitionSpec as P
from jax.experimental import pallas as pl
from jax.experimental.pallas import tpu as pltpu

couple_rate = 0.1
time_step = 0.2
LANES = 128
GROUP = 4
VMEM_LIMIT = 48 * 1024 * 1024


def neighbours(block, axis):
    count = lax.axis_size(axis)
    forward = [(i, i + 1) for i in range(count - 1)]
    backward = [(target, source) for source, target in forward]
    return lax.ppermute(block, axis, forward), lax.ppermute(block, axis, backward)


def flow_kernel(cell_ref, rate_ref, disp_ref, state_out, slab_out, prev_out, next_out,
                held, crest_edge, crest_halo, plan_halo,
                crest_send, crest_recv, plan_send, plan_recv, disp_send, disp_recv,
                slab_send, slab_recv):
    x, y = lax.axis_index("gx"), lax.axis_index("gy")
    nx, ny = lax.axis_size("gx"), lax.axis_size("gy")
    rows, layers, crest, thick = cell_ref.shape
    slab = layers // ny
    has_lo, has_hi = (x > 0, y > 0), (x < nx - 1, y < ny - 1)

    barrier = pltpu.get_barrier_semaphore()

    def greet(axis, target):
        pl.semaphore_signal(barrier, inc=1, device_id={axis: target},
                            device_id_type=pl.DeviceIdType.MESH)

    @pl.when(has_lo[0])
    def _():
        greet("gx", x - 1)

    @pl.when(has_hi[0])
    def _():
        greet("gx", x + 1)

    for o in range(1, ny):
        greet("gy", lax.rem(y + o, ny))
    greeted = jnp.where(has_lo[0], 1, 0) + jnp.where(has_hi[0], 1, 0) + (ny - 1)
    pl.semaphore_wait(barrier, greeted)

    def remote(src, dst, send, recv, axis, target):
        return pltpu.make_async_remote_copy(
            src_ref=src, dst_ref=dst, send_sem=send, recv_sem=recv,
            device_id={axis: target}, device_id_type=pl.DeviceIdType.MESH)

    def both_ways(axis, lo_src, hi_src, lo_dst, hi_dst, send, recv):
        at, i = (x, 0) if axis == "gx" else (y, 1)
        down = remote(lo_src, hi_dst, send.at[0], recv.at[0], axis, at - 1)
        up = remote(hi_src, lo_dst, send.at[1], recv.at[1], axis, at + 1)
        return has_lo[i], has_hi[i], down, up, lo_dst, hi_dst

    def start(pair):
        lo, hi, down, up, lo_dst, hi_dst = pair

        @pl.when(lo)
        def _():
            down.start()

        @pl.when(hi)
        def _():
            up.start()

        @pl.when(jnp.logical_not(lo))
        def _():
            lo_dst[...] = jnp.zeros_like(lo_dst)

        @pl.when(jnp.logical_not(hi))
        def _():
            hi_dst[...] = jnp.zeros_like(hi_dst)

    def finish(pair):
        lo, hi, down, up, _, _ = pair

        @pl.when(lo)
        def _():
            down.wait_send()
            up.wait_recv()

        @pl.when(hi)
        def _():
            up.wait_send()
            down.wait_recv()

    states = [cell_ref, held.at[0], held.at[1], state_out]
    lane = lax.broadcasted_iota(jnp.int32, (crest, thick), 1)
    line = lax.broadcasted_iota(jnp.int32, (crest, thick), 0)
    whole = (crest, thick)
    disp_pair = both_ways("gx", disp_ref, disp_ref, prev_out, next_out, disp_send, disp_recv)
    for step in range(3):
        now, later = states[step], states[step + 1]
        for r in range(rows):
            for l in range(layers):
                crest_edge[step, 0, r, l:l + 1, :] = now[r, l, 0:1, :]
                crest_edge[step, 1, r, l:l + 1, :] = now[r, l, crest - 1:crest, :]
        crest_pair = both_ways("gx", crest_edge.at[step, 0], crest_edge.at[step, 1],
                               crest_halo.at[step, 0], crest_halo.at[step, 1],
                               crest_send.at[step], crest_recv.at[step])
        plan_pair = both_ways("gy", now.at[:, :, :, 0:LANES], now.at[:, :, :, thick - LANES:thick],
                              plan_halo.at[step, 0], plan_halo.at[step, 1],
                              plan_send.at[step], plan_recv.at[step])
        start(plan_pair)
        start(crest_pair)
        if step == 0:
            start(disp_pair)
        finish(plan_pair)
        finish(crest_pair)
        for l in range(layers):
            center = [now[r, l] for r in range(rows)]
            for r in range(rows):
                c = center[r]
                none = jnp.zeros_like(c)
                lap = (now[r, l + 1] if l + 1 < layers else none) + (now[r, l - 1] if l > 0 else none)
                lap += jnp.where(line == crest - 1,
                                 jnp.broadcast_to(crest_halo[step, 1, r, l:l + 1, :], whole),
                                 pltpu.roll(c, crest - 1, 0))
                lap += jnp.where(line == 0,
                                 jnp.broadcast_to(crest_halo[step, 0, r, l:l + 1, :], whole),
                                 pltpu.roll(c, 1, 0))
                hi_col = plan_halo[step, 1, r, l][:, 0:1]
                lo_col = plan_halo[step, 0, r, l][:, LANES - 1:LANES]
                lap += jnp.where(lane == thick - 1, jnp.broadcast_to(hi_col, whole),
                                 pltpu.roll(c, thick - 1, 1))
                lap += jnp.where(lane == 0, jnp.broadcast_to(lo_col, whole), pltpu.roll(c, 1, 1))
                lap -= 6.0 * c
                later[r, l] = c + rate_ref[r, l] * lap + couple_rate * (center[1 - r] - c)

    copies = []
    for o in range(1, ny):
        target = lax.rem(y + o, ny)
        copies.append(remote(state_out.at[:, pl.ds(target * slab, slab)], slab_out.at[y],
                             slab_send.at[o - 1], slab_recv.at[o - 1], "gy", target))
    for copy in copies:
        copy.start()
    slab_out[y] = state_out[:, pl.ds(y * slab, slab)]
    for copy in copies:
        copy.wait()
    finish(disp_pair)


WIDE = 1024


def stage_rows(staged, sources, first, total):
    base = 0
    for ref in sources:
        rows = ref.shape[0]
        if len(ref.shape) == 3:
            count = ref.shape[1]
            for r in range(rows):
                at = (first + r) * total + base
                staged[at:at + count, :] = ref[r]
        else:
            count = ref.shape[1] // LANES
            for h in range(count):
                staged[pl.ds(first * total + base + h, rows, stride=total), :] = (
                    ref[:, h * LANES:(h + 1) * LANES])
        base += count


def split_table(table, staged):
    value = staged[...]
    top = value.astype(jnp.bfloat16)
    table[:, 0:LANES] = top
    table[:, LANES:2 * LANES] = (value - top.astype(jnp.float32)).astype(jnp.bfloat16)


def look(table, rows, index_row, out, at):
    total = table.shape[0] // rows
    low = jnp.broadcast_to(jnp.bitwise_and(index_row, LANES - 1), (LANES, WIDE))
    hot = jnp.where(low == lax.broadcasted_iota(jnp.int32, (LANES, WIDE), 0), 1.0, 0.0)
    hot = hot.astype(jnp.bfloat16)
    found = jnp.dot(table[...], jnp.concatenate([hot, hot], axis=0), preferred_element_type=jnp.float32)
    high = jnp.broadcast_to(lax.shift_right_logical(index_row, 7), (8, WIDE))
    high = high - lax.broadcasted_iota(jnp.int32, (8, WIDE), 0)
    acc = [jnp.zeros((8, WIDE), jnp.float32) for _ in range(rows)]
    for hb in range(total // 8):
        mask = high == 8 * hb
        for r in range(rows):
            first = r * total + 8 * hb
            acc[r] = jnp.where(mask, found[first:first + 8, :], acc[r])
    for r in range(rows):
        for k in range(WIDE // LANES):
            out[r, pl.ds(at + 8 * k, 8), :] = acc[r][:, k * LANES:(k + 1) * LANES]


def index_of(ref, g):
    per = WIDE // LANES
    return jnp.concatenate([ref[pl.ds(g * per + k, 1), :] for k in range(per)], axis=1)


def gathered_row(out, r, first, count):
    parts = [out[r, pl.ds(first * 8 + s, count, stride=8), :] for s in range(8)]
    while len(parts) > 1:
        parts = [x + y for x, y in zip(parts[::2], parts[1::2])]
    return parts[0]


def cross(left, right):
    return [
        left[1] * right[2] - left[2] * right[1],
        left[2] * right[0] - left[0] * right[2],
        left[0] * right[1] - left[1] * right[0],
    ]


def call(kernel, outs, scratch=(), smem=0, count=0, cost=None):
    specs = [pl.BlockSpec(memory_space=pltpu.SMEM)] * smem
    specs += [pl.BlockSpec(memory_space=pltpu.VMEM)] * (count - smem)
    return pl.pallas_call(
        kernel,
        out_shape=outs,
        in_specs=specs,
        out_specs=jax.tree.map(lambda _: pl.BlockSpec(memory_space=pltpu.VMEM), outs),
        scratch_shapes=list(scratch),
        compiler_params=pltpu.CompilerParams(vmem_limit_bytes=VMEM_LIMIT),
        cost_estimate=cost,
    )


def host_kernel(slab_ref, host_ref, out_ref, staged, table, found):
    sources, _, layers, crest, thick = slab_ref.shape
    pieces = thick // LANES
    line = sources * pieces
    for j in range(sources):
        for r in range(2):
            for l in range(layers):
                for p in range(pieces):
                    at = ((r * layers + l) * crest) * line + j * pieces + p
                    staged[pl.ds(at, crest, stride=line), :] = (
                        slab_ref[j, r, l, :, p * LANES:(p + 1) * LANES])
    split_table(table, staged)

    def chunk(g, carry):
        look(table, 2, index_of(host_ref, g), found, pl.multiple_of(g * 8 * (WIDE // LANES), 8))
        return carry

    blocks = host_ref.shape[0]
    lax.fori_loop(0, blocks * LANES // WIDE, chunk, 0)
    for r in range(2):
        out_ref[r] = gathered_row(found, r, 0, blocks)


def unpack(src, k0, rows, stage):
    for k in range(8 * GROUP):
        at = pl.multiple_of((k0 + k) * LANES, LANES)
        stage[k * rows:(k + 1) * rows, :] = src[:, pl.ds(at, LANES)]
    return [stage[pl.ds(m, 8 * GROUP, stride=rows), :] for m in range(rows)]


def find_both(own_ref, other_ref, owners, windows, scratch):
    staged_a, table_a, found_a, staged_b, table_b, found_b = scratch
    rows = sum(ref.shape[0] for ref in owners)
    first = 0
    for ref, three in zip(owners, windows):
        stage_rows(staged_a, [ref], first, staged_a.shape[0] // rows)
        stage_rows(staged_b, three, first, staged_b.shape[0] // rows)
        first += ref.shape[0]
    split_table(table_a, staged_a)
    split_table(table_b, staged_b)

    def chunk(g, carry):
        at = pl.multiple_of(g * 8 * (WIDE // LANES), 8)
        look(table_a, rows, index_of(own_ref, g), found_a, at)
        look(table_b, rows, index_of(other_ref, g), found_b, at)
        return carry

    lax.fori_loop(0, own_ref.shape[0] * LANES // WIDE, chunk, 0)
    return found_a, found_b


def delta_at(found_a, found_b, arms_ref, out_ref, stage, at):
    a = [gathered_row(found_a, r, at, 8 * GROUP) for r in range(6)]
    b = [gathered_row(found_b, r, at, 8 * GROUP) for r in range(6)]
    arms = unpack(arms_ref, at, 6, stage)
    turn_a = cross(a[3:6], arms[0:3])
    turn_b = cross(b[3:6], arms[3:6])
    for m in range(3):
        out_ref[m, pl.ds(at, 8 * GROUP), :] = (b[m] + turn_b[m]) - (a[m] + turn_a[m])


def first_kernel(own_q, prev_q, next_q, own_f, prev_f, next_f, own_ref, other_ref, arms_ref,
                 eigen_ref, out_ref, eig_ref, stage, *scratch):
    found_a, found_b = find_both(own_ref, other_ref, [own_q, own_f],
                                 [[prev_q, own_q, next_q], [prev_f, own_f, next_f]], scratch)

    def chunk(g, carry):
        at = pl.multiple_of(g * 8 * GROUP, 8 * GROUP)
        delta_at(found_a, found_b, arms_ref, out_ref, stage, at)
        eig = unpack(eigen_ref, at, 2, stage)
        pore, heat = [
            gathered_row(found_a, r, at, 8 * GROUP) + gathered_row(found_b, r, at, 8 * GROUP)
            for r in (6, 7)]
        eig_ref[pl.ds(at, 8 * GROUP), :] = 0.5 * (eig[0] * heat + eig[1] * pore)
        return carry

    lax.fori_loop(0, own_ref.shape[0] // (8 * GROUP), chunk, 0)


def delta_kernel(own_q, prev_q, next_q, own_ref, other_ref, arms_ref, out_ref, stage, *scratch):
    found_a, found_b = find_both(own_ref, other_ref, [own_q], [[prev_q, own_q, next_q]], scratch)

    def chunk(g, carry):
        delta_at(found_a, found_b, arms_ref, out_ref, stage, pl.multiple_of(g * 8 * GROUP, 8 * GROUP))
        return carry

    lax.fori_loop(0, own_ref.shape[0] // (8 * GROUP), chunk, 0)


def update_kernel(live_ref, delta_ref, eig_ref, own_ref, arms_ref, frame_ref, stiff_ref,
                  inertia_ref, disp_ref, vel_ref, disp_out, vel_out,
                  stage, terms, amat, bmat, total):
    blocks = own_ref.shape[0]
    parts = disp_ref.shape[1]
    low_count = 2 * LANES
    high_count = parts // low_count
    per = 8 * GROUP
    live = live_ref[0]
    total[...] = jnp.zeros_like(total)

    def chunk(g, carry):
        at = pl.multiple_of(g * per, per)
        rows = pl.ds(at, per)
        frame = unpack(frame_ref, at, 9, stage)
        delta = [delta_ref[m, rows, :] for m in range(3)]
        e = [frame[3 * k] * delta[0] + frame[3 * k + 1] * delta[1] + frame[3 * k + 2] * delta[2]
             for k in range(3)]
        stiff = unpack(stiff_ref, at, 2, stage)
        block = at + lax.broadcasted_iota(jnp.int32, (per, LANES), 0)
        weight = jnp.where(block < live, 1.0, 0.0).astype(jnp.float32)
        s = [stiff[0] * (e[0] - eig_ref[rows, :]), stiff[1] * e[1], stiff[1] * e[2]]
        force = [(s[0] * frame[m] + s[1] * frame[3 + m] + s[2] * frame[6 + m]) * weight
                 for m in range(3)]
        arms = unpack(arms_ref, at, 6, stage)
        moment = cross(arms[0:3], force)
        for m in range(3):
            terms[m] = force[m]
            terms[3 + m] = moment[m]

        low_iota = lax.broadcasted_iota(jnp.int32, (low_count, LANES), 0)
        high_iota = lax.broadcasted_iota(jnp.int32, (high_count, LANES), 0)
        for k in range(per):
            lanes = pl.ds(k * LANES, LANES)
            ix = own_ref[pl.ds(at + k, 1), :]
            low = jnp.broadcast_to(jnp.bitwise_and(ix, low_count - 1), (low_count, LANES))
            bmat[:, lanes] = jnp.where(low == low_iota, 1.0, 0.0).astype(jnp.bfloat16)
            here = jnp.broadcast_to(lax.shift_right_logical(ix, 8), (high_count, LANES)) == high_iota
            for m in range(6):
                row = terms[m, k:k + 1, :]
                top = row.astype(jnp.bfloat16).astype(jnp.float32)
                rest = row - top
                at_m = m * high_count
                amat[at_m:at_m + high_count, lanes] = jnp.where(
                    here, jnp.broadcast_to(top, here.shape), 0.0).astype(jnp.bfloat16)
                at_m = (6 + m) * high_count
                amat[at_m:at_m + high_count, lanes] = jnp.where(
                    here, jnp.broadcast_to(rest, here.shape), 0.0).astype(jnp.bfloat16)
        total[...] += lax.dot_general(amat[...], bmat[...], (((1,), (1,)), ((), ())),
                                      preferred_element_type=jnp.float32)
        return carry

    lax.fori_loop(0, blocks // per, chunk, 0)
    half = 6 * high_count
    total[0:half, :] = total[0:half, :] + total[half:2 * half, :]
    for h in range(high_count):
        lanes = pl.ds(h * low_count, low_count)
        load = jnp.concatenate([total[m * high_count + h:m * high_count + h + 1, :] for m in range(6)], axis=0)
        mass = jnp.concatenate([jnp.broadcast_to(inertia_ref[0:1, lanes], (3, low_count)),
                                jnp.broadcast_to(inertia_ref[1:2, lanes], (3, low_count))], axis=0)
        vel = vel_ref[:, lanes] + time_step * load / mass
        vel_out[:, lanes] = vel
        disp_out[:, lanes] = disp_ref[:, lanes] + time_step * vel


def body(
    cell_start,
    diffusivity,
    host_cell,
    disp_start,
    vel_start,
    inertia,
    facet_own,
    facet_other,
    facet_arms,
    facet_frame,
    facet_stiffness,
    facet_eigen,
    live_blocks,
):
    f32 = jnp.float32
    facets = facet_own.shape[0]
    blocks = facets // LANES
    particles = disp_start.shape[1]
    own = facet_own.reshape(blocks, LANES)
    other = facet_other.reshape(blocks, LANES)
    per = 8 * GROUP

    ny = lax.axis_size("gy")
    rows, layers, crest, thick = cell_start.shape
    dma = pltpu.SemaphoreType.DMA
    shape = lambda *dims: jax.ShapeDtypeStruct(dims, f32)
    vmem = pl.BlockSpec(memory_space=pltpu.VMEM)
    state, slab, prev_q, next_q = pl.pallas_call(
        flow_kernel,
        out_shape=(shape(*cell_start.shape), shape(ny, rows, layers // ny, crest, thick),
                   shape(*disp_start.shape), shape(*disp_start.shape)),
        in_specs=[vmem] * 3,
        out_specs=(vmem,) * 4,
        scratch_shapes=[
            pltpu.VMEM((2,) + cell_start.shape, f32),
            pltpu.VMEM((3, 2, rows, layers, thick), f32),
            pltpu.VMEM((3, 2, rows, layers, thick), f32),
            pltpu.VMEM((3, 2, rows, layers, crest, LANES), f32),
            dma((3, 2)), dma((3, 2)), dma((3, 2)), dma((3, 2)), dma((2,)), dma((2,)),
            dma((ny - 1,)), dma((ny - 1,)),
        ],
        compiler_params=pltpu.CompilerParams(
            vmem_limit_bytes=VMEM_LIMIT, collective_id=0, has_side_effects=True),
    )(cell_start, diffusivity, disp_start)

    def tables(rows, high, found):
        return [pltpu.VMEM((rows * high, LANES), f32),
                pltpu.VMEM((rows * high, 2 * LANES), jnp.bfloat16),
                pltpu.VMEM((rows, 8 * found, LANES), f32)]

    high = particles // LANES
    fields = call(host_kernel, jax.ShapeDtypeStruct((2, high, LANES), f32), count=2,
                  scratch=tables(2, slab.size // (2 * LANES), high))(
        slab, host_cell.reshape(-1, LANES))
    prev_f, next_f = neighbours(fields, "gx")
    delta, eig = call(first_kernel, (shape(3, blocks, LANES), shape(blocks, LANES)), count=10,
                      scratch=[pltpu.VMEM((per * 6, LANES), f32)] + tables(8, high, blocks)
                      + tables(8, 3 * high, blocks))(
        disp_start, prev_q, next_q, fields, prev_f, next_f, own, other, facet_arms, facet_eigen)

    disp, vel = disp_start, vel_start
    high_count = particles // (2 * LANES)
    for substep in range(2):
        if substep > 0:
            prev_q, next_q = neighbours(disp, "gx")
            delta = call(delta_kernel, jax.ShapeDtypeStruct((3, blocks, LANES), f32), count=6,
                         scratch=[pltpu.VMEM((per * 6, LANES), f32)] + tables(6, high, blocks)
                         + tables(6, 3 * high, blocks))(
                disp, prev_q, next_q, own, other, facet_arms)
        disp, vel = call(
            update_kernel,
            (jax.ShapeDtypeStruct(disp.shape, f32), jax.ShapeDtypeStruct(vel.shape, f32)),
            count=10, smem=1,
            scratch=[
                pltpu.VMEM((per * 9, LANES), f32),
                pltpu.VMEM((6, per, LANES), f32),
                pltpu.VMEM((12 * high_count, per * LANES), jnp.bfloat16),
                pltpu.VMEM((2 * LANES, per * LANES), jnp.bfloat16),
                pltpu.VMEM((12 * high_count, 2 * LANES), f32),
            ])(live_blocks, delta, eig, own, facet_arms, facet_frame, facet_stiffness,
               inertia, disp, vel)
    return (state, disp, vel)


def solution(mesh):
    cells = P(None, None, ("groups", "gx"), "gy")
    vector = P(("groups", "gx", "gy"))
    rows = P(None, ("groups", "gx", "gy"))
    return jax.shard_map(
        body,
        mesh=mesh,
        in_specs=(cells, cells, vector, rows, rows, rows, vector, vector, rows, rows, rows, rows,
                  vector),
        out_specs=(cells, rows, rows),
        check_vma=False,
    )
```
